32 devices in a mesh: replica: 4 (over x, core), fsdp: 8 (over z, y).
Axes of the slice: x: 2, y: 2, z: 4, core: 2. Of those that a mesh axis runs over, the one named last changes fastest.
Arguments:
- tokens: bfloat16 [8192, 2048], P(('replica', 'fsdp')), may hold values from -6 to 6
- inner_q: bfloat16 [4, 2048, 2048], P('replica', 'fsdp')
- inner_k: bfloat16 [4, 2048, 512], P('replica', 'fsdp')
- inner_v: bfloat16 [4, 2048, 512], P('replica', 'fsdp')
- outer_q: float32 [2048, 2048], P('fsdp')
- outer_k: float32 [2048, 512], P('fsdp')
- outer_v: float32 [2048, 512], P('fsdp')
- moment_q: float32 [2048, 2048], P('fsdp', 'replica'), may hold values from -0.09375 to 0.09375
- moment_k: float32 [2048, 512], P('fsdp', 'replica'), may hold values from -0.09375 to 0.09375
- value_momentum: float32 [2048, 512], P('fsdp', 'replica'), may hold values from -0.09375 to 0.09375
Outputs:
- projected: bfloat16 [8192, 3072], P(('replica', 'fsdp'))
- updated_outer_query: float32 [2048, 2048], P('fsdp')
- updated_outer_key: float32 [2048, 512], P('fsdp')
- new_outer_v: float32 [2048, 512], P('fsdp')
- new_moment_q: float32 [2048, 2048], P('fsdp', 'replica')
- new_moment_k: float32 [2048, 512], P('fsdp', 'replica')
- new_moment_v: float32 [2048, 512], P('fsdp', 'replica')
The draws below stay inside these ranges and needn't reach their ends.
All inputs are finite; a program needn't handle non-finite values.
Results may differ from the reference program's by a relative error of at most 0.005.
Values may be sent and summed in bfloat16 or wider, within the bound.
No kernel may reach another device: no remote copies, remote signals or barrier semaphores. Data moves between devices by JAX's collectives and lax.ppermute only.
A program may use at most 64 MiB of HBM per device.

```python
import jax
import jax.numpy as jnp

D = 2048
HQ = 32
KEY_VALUE_HEADS = 8
HEAD_SIZE = 64
QCOLS = 2048
KVCOLS = 512
TOKENS = 8192
N_REPLICA = 4


def unit_noise(key, shape):
    return jnp.clip(jax.random.normal(key, shape, jnp.float32), -6.0, 6.0)


def outer_starting_weight(key, salt, columns):
    return unit_noise(jax.random.fold_in(key, salt), (D, columns)) / jnp.sqrt(jnp.float32(D))


def inner_weights_from(key, salt, columns):
    base = outer_starting_weight(key, salt, columns)
    drift = unit_noise(jax.random.fold_in(key, salt + 100), (N_REPLICA, D, columns))
    return (base[None] + 0.3 * drift / jnp.sqrt(jnp.float32(D))).astype(jnp.bfloat16)


def draw_outer_q(key, part):
    return outer_starting_weight(key, 1, HQ * HEAD_SIZE)


def draw_outer_k(key, part):
    return outer_starting_weight(key, 2, KEY_VALUE_HEADS * HEAD_SIZE)


def draw_outer_v(key, part):
    return outer_starting_weight(key, 3, KEY_VALUE_HEADS * HEAD_SIZE)


def draw_inner_q(key, part):
    return inner_weights_from(key, 1, HQ * HEAD_SIZE)


def draw_inner_k(key, part):
    return inner_weights_from(key, 2, KEY_VALUE_HEADS * HEAD_SIZE)


def draw_inner_v(key, part):
    return inner_weights_from(key, 3, KEY_VALUE_HEADS * HEAD_SIZE)


def block_scale(rng, dims, shards, least, top_value):
    def one(dim, blocks):
        steps = jax.random.uniform(jax.random.fold_in(jax.random.fold_in(rng, 6), dim), (blocks,), jnp.float32, least / len(shards), top_value / len(shards))
        return jnp.repeat(jnp.exp(steps), dims[dim] // blocks).reshape((-1,) + (1,) * (len(dims) - dim - 1))

    level = one(*shards[0])
    for cut in shards[1:]:
        level = level * one(*cut)
    return level


def normal_values(key, shape, scale, bound, cuts=(), dtype=jnp.bfloat16):
    entries = jax.random.normal(key, shape, jnp.float32) * scale
    if len(cuts) > 0:
        entries = block_scale(key, shape, cuts, -0.22, 0.18) * entries
    return jnp.clip(entries, min=-bound, max=bound).astype(dtype)


def setup_inputs(seed: int = 0) -> dict:
    splits = jax.random.split(jax.random.key(seed), 11)
    return {
        "tokens": normal_values(splits[0], (TOKENS, D), 1.0, 6.0, ((0, 32),)),
        "inner_q": draw_inner_q(jax.random.fold_in(splits[10], 71), 0),
        "inner_k": draw_inner_k(jax.random.fold_in(splits[10], 71), 0),
        "inner_v": draw_inner_v(jax.random.fold_in(splits[10], 71), 0),
        "outer_q": draw_outer_q(jax.random.fold_in(splits[10], 71), 0),
        "outer_k": draw_outer_k(jax.random.fold_in(splits[10], 71), 0),
        "outer_v": draw_outer_v(jax.random.fold_in(splits[10], 71), 0),
        "moment_q": normal_values(splits[7], (D, QCOLS), (0.3 / D ** 0.5), 0.09375, ((0, 8), (1, 4)), jnp.float32),
        "moment_k": normal_values(splits[8], (D, KVCOLS), (0.3 / D ** 0.5), 0.09375, ((0, 8), (1, 4)), jnp.float32),
        "value_momentum": normal_values(splits[9], (D, KVCOLS), (0.3 / D ** 0.5), 0.09375, ((0, 8), (1, 4)), jnp.float32),
    }


def outer_step(inner, outer, outer_momentum):
    pseudo = jnp.sum(outer[None] - inner.astype(jnp.float32), axis=0) / N_REPLICA
    new_moment = 0.9 * outer_momentum + pseudo
    new_outer = outer - 0.7 * (pseudo + 0.9 * new_moment)
    return new_outer, new_moment


def reference(tokens, inner_q, inner_k, inner_v, outer_q, outer_k, outer_v, moment_q, moment_k, value_momentum):
    updated_outer_query, new_moment_q = outer_step(inner_q, outer_q, moment_q)
    updated_outer_key, new_moment_k = outer_step(inner_k, outer_k, moment_k)
    new_outer_v, new_moment_v = outer_step(inner_v, outer_v, value_momentum)
    fresh = jnp.concatenate([updated_outer_query, updated_outer_key, new_outer_v], axis=1).astype(jnp.bfloat16)
    projected = jnp.dot(tokens, fresh, preferred_element_type=jnp.float32).astype(jnp.bfloat16)
    return projected, updated_outer_query, updated_outer_key, new_outer_v, new_moment_q, new_moment_k, new_moment_v
```

```python
import functools

import jax
import jax.numpy as jnp
from jax import lax
from jax.experimental import pallas as pl
from jax.experimental.pallas import tpu as pltpu
from jax.sharding import PartitionSpec as P

LEARN_RATE = 0.7
MOMENTUM_BETA = 0.9
SMALL_VMEM = 12 * 1024 * 1024
LONGEST_RING = 16


def from_replica(x, distance):
    count = lax.axis_size("replica")
    return lax.ppermute(x, "replica", [(i, i ^ distance) for i in range(count)])


def ring_member(p, n):
    return 2 * p if p < n // 2 else 2 * (n - 1 - p) + 1


def source_of(row, steps, n):
    p = jnp.where(row % 2 == 0, row // 2, n - 1 - row // 2)
    p = (p - steps + n) % n
    return jnp.where(p < n // 2, 2 * p, 2 * (n - 1 - p) + 1)


def after(x, *others):
    return lax.optimization_barrier((x, *others))[0]


def fetch(sources, buffers, sems):
    copies = [pltpu.make_async_copy(a, b, sems.at[i]) for i, (a, b) in enumerate(zip(sources, buffers))]
    for copy in copies:
        copy.start()
    for copy in copies:
        copy.wait()


def columns_at(ref, block, width):
    return ref.at[:, pl.ds(pl.multiple_of(block * width, width), width)]


def in_hbm(arrays):
    return [pltpu.with_memory_space_constraint(a, pltpu.HBM) for a in arrays]


def blocks_of(arrays, widths):
    return [pltpu.VMEM((a.shape[0], w), a.dtype) for a, w in zip(arrays, widths * 3)]


def spread(pieces, outs):
    edges = [0]
    for piece in pieces:
        edges.append(edges[-1] + piece.shape[1])
    left = 0
    for out in outs:
        right = left + out.shape[1]
        for piece, start in zip(pieces, edges):
            low, high = max(left, start), min(right, start + piece.shape[1])
            if low < high:
                out[:, low - left : high - left] = piece[:, low - start : high - start].astype(out.dtype)
        left = right


def pair_sums(inners, siblings, outers):
    sums = []
    for inner, sibling, outer in zip(inners, siblings, outers):
        base = outer[...]
        sums.append(base + base - (inner[...].astype(jnp.float32) + sibling[...].astype(jnp.float32)))
    return sums


def far_kernel(where, *refs):
    sources, outs, buffers, sems = refs[:9], refs[9:11], refs[11:20], refs[20]
    block = lax.bitwise_xor(where[0], 2)
    fetch([columns_at(r, block, b.shape[1]) for r, b in zip(sources, buffers)], buffers, sems)
    spread(pair_sums(buffers[:3], buffers[3:6], buffers[6:]), outs)


def near_kernel(where, *refs):
    sources, moments = refs[:9], refs[9:12]
    sums, own, packed, buffers, sems = refs[12:14], refs[14:16], refs[16:18], refs[18:27], refs[27]
    fetch([columns_at(r, where[0], b.shape[1]) for r, b in zip(sources, buffers)], buffers, sems)
    spread(pair_sums(buffers[:3], buffers[3:6], buffers[6:]), sums)
    spread(buffers[6:], own)
    spread(moments, packed)


def sums_call(kernel, where, inners, siblings, outers, moments, widths, shapes, name):
    arrays = (*inners, *siblings, *outers)
    return pl.pallas_call(
        kernel,
        out_shape=shapes,
        in_specs=[pl.BlockSpec(memory_space=pltpu.SMEM)]
        + [pl.BlockSpec(memory_space=pl.ANY)] * 9
        + [pl.BlockSpec(memory_space=pltpu.VMEM)] * len(moments),
        out_specs=[pl.BlockSpec(memory_space=pltpu.VMEM)] * len(shapes),
        scratch_shapes=[*blocks_of(arrays, widths), pltpu.SemaphoreType.DMA((9,))],
        compiler_params=pltpu.CompilerParams(vmem_limit_bytes=SMALL_VMEM),
        name=name,
    )(where, *in_hbm(inners), *siblings, *in_hbm(outers), *moments)


def subtract_kernel(where, outer_q, outer_k, outer_v, *refs):
    deltas, outs = refs[:-3], refs[-3:]
    outers = (outer_q, outer_k, outer_v)
    me = where[0]
    for distance, delta in enumerate(deltas):
        block = lax.bitwise_xor(me, distance)
        start = 0
        for outer, out in zip(outers, outs):
            width = outer.shape[1] // len(deltas)
            columns = pl.ds(pl.multiple_of(block * width, width), width)
            out[:, columns] = outer[:, columns] - delta[:, start : start + width].astype(jnp.float32)
            start += width


def subtract(where, outers, deltas):
    return pl.pallas_call(
        subtract_kernel,
        out_shape=[jax.ShapeDtypeStruct(o.shape, o.dtype) for o in outers],
        in_specs=[pl.BlockSpec(memory_space=pltpu.SMEM)]
        + [pl.BlockSpec(memory_space=pltpu.VMEM)] * (len(outers) + len(deltas)),
        out_specs=[pl.BlockSpec(memory_space=pltpu.VMEM)] * len(outers),
        compiler_params=pltpu.CompilerParams(vmem_limit_bytes=SMALL_VMEM),
        name="outer_minus_delta",
    )(where, *outers, *deltas)


def place_kernel(widths, where, *refs):
    sources, out = refs[:-1], refs[-1]
    count = len(sources) // 2
    for distance in range(count):
        block = lax.bitwise_xor(where[0], distance)
        targets, start = [], 0
        for width in widths:
            targets.append(out.at[:, pl.ds(pl.multiple_of(start + block * width, width), width)])
            start += count * width
        spread(sources[2 * distance : 2 * distance + 2], targets)


def place(where, pieces, widths):
    parts = [part for piece in pieces for part in piece]
    return pl.pallas_call(
        functools.partial(place_kernel, widths),
        out_shape=jax.ShapeDtypeStruct((parts[0].shape[0], len(pieces) * sum(widths)), jnp.bfloat16),
        in_specs=[pl.BlockSpec(memory_space=pltpu.SMEM)]
        + [pl.BlockSpec(memory_space=pltpu.VMEM)] * len(parts),
        out_specs=pl.BlockSpec(memory_space=pltpu.VMEM),
        compiler_params=pltpu.CompilerParams(vmem_limit_bytes=SMALL_VMEM),
        name="place_columns",
    )(where, *parts)


def per_device(
    tokens, inner_q, inner_k, inner_v, outer_q, outer_k, outer_v, moment_q, moment_k, value_momentum
):
    count = lax.axis_size("replica")
    n = lax.axis_size("fsdp")
    me = lax.axis_index("replica")
    row = lax.axis_index("fsdp")
    inners = (inner_q[0], inner_k[0], inner_v[0])
    outers = (outer_q, outer_k, outer_v)
    moments = (moment_q, moment_k, value_momentum)
    widths = [m.shape[1] for m in moments]
    rows = outer_q.shape[0]
    mine = tokens.shape[0]
    total_width = sum(widths)
    streams = (total_width // 2, total_width - total_width // 2)

    def shapes(dtype):
        return [jax.ShapeDtypeStruct((rows, w), dtype) for w in streams]

    where = me.astype(jnp.int32).reshape(1)
    siblings = [from_replica(a, 1) for a in inners]
    fars = sums_call(far_kernel, where, inners, siblings, outers, (), widths, shapes(jnp.bfloat16), "far_sums")
    remotes = [from_replica(far, 2) for far in fars]
    near = sums_call(
        near_kernel, where, inners, siblings, outers, moments, widths, shapes(jnp.float32) * 3, "near_sums"
    )
    fresh, deltas, new_moments = [], [], []
    for own, outer, moment, remote in zip(near[:2], near[2:4], near[4:], remotes):
        pseudo = (own + remote.astype(jnp.float32)) / count
        new_moment = MOMENTUM_BETA * moment + pseudo
        delta = LEARN_RATE * (pseudo + MOMENTUM_BETA * new_moment)
        fresh.append((outer - delta).astype(jnp.bfloat16))
        deltas.append(delta.astype(jnp.bfloat16))
        new_moments.append(new_moment)

    tokens_1 = from_replica(after(tokens, *fars), 1)
    tokens_2 = from_replica(after(tokens, *remotes), 2)
    near_tokens = jnp.concatenate([tokens, tokens_1], axis=0)

    up = [(ring_member(p, n), ring_member((p + 1) % n, n)) for p in range(n)]
    down = [(b, a) for a, b in up]
    more, less = n // 2, n - 1 - n // 2

    def product(lhs, steps, block):
        lanes = lax.dynamic_slice_in_dim(lhs, source_of(row, steps, n) * rows, rows, 1)
        return jnp.dot(lanes, block, preferred_element_type=jnp.float32)

    delta = jnp.concatenate(deltas, axis=1)
    arrived = [[(0, part)] for part in fresh]
    near_totals = [product(near_tokens, 0, part) for part in fresh]
    if n > LONGEST_RING:
        gathered = [lax.all_gather(part, "fsdp", axis=0, tiled=True) for part in fresh]
        tokens_3 = from_replica(tokens_2, 1)
        far_tokens = jnp.concatenate([tokens_2, tokens_3], axis=0)
        delta_2 = from_replica(after(delta, tokens_3), 2)
        near_totals = [jnp.dot(near_tokens, g, preferred_element_type=jnp.float32) for g in gathered]
        far_totals = [jnp.dot(far_tokens, g, preferred_element_type=jnp.float32) for g in gathered]
    else:
        ups, downs = list(fresh), list(fresh)
        limits = ((more, less), (less, more))
        far_totals = [None] * len(fresh)
        for step in range(1, more + 1):
            for index, (up_limit, down_limit) in enumerate(limits):
                before = near_totals[index]
                if step <= up_limit:
                    ups[index] = lax.ppermute(after(ups[index], before), "fsdp", up)
                    arrived[index].append((step, ups[index]))
                if step <= down_limit:
                    downs[index] = lax.ppermute(after(downs[index], before), "fsdp", down)
                    arrived[index].append((-step, downs[index]))
                if step == more:
                    far_totals[index] = sum(product(far_tokens, *a) for a in arrived[index][:-1])
                    arrived[index][-1] = (arrived[index][-1][0], after(arrived[index][-1][1], far_totals[index], delta_2))
                    far_totals[index] += product(far_tokens, *arrived[index][-1])
                for a in arrived[index][2 * step - 1 :]:
                    near_totals[index] += product(near_tokens, *a)
            if step == 2:
                tokens_2 = after(tokens_2, ups[1])
                tokens_3 = from_replica(tokens_2, 1)
                far_tokens = jnp.concatenate([tokens_2, tokens_3], axis=0)
                delta_2 = from_replica(after(delta, tokens_3), 2)

    pieces = [[], [], [], []]
    for near_total, far_total in zip(near_totals, far_totals):
        out = near_total.astype(jnp.bfloat16)
        far_out = far_total.astype(jnp.bfloat16)
        pieces[2].append(from_replica(far_out[:mine], 2))
        pieces[3].append(from_replica(far_out[mine:], 3))
        pieces[0].append(out[:mine])
        pieces[1].append(from_replica(out[mine:], 1))

    delta_1 = from_replica(after(delta, delta_2), 1)
    delta_3 = from_replica(after(delta_2, delta_1), 1)
    new_outers = subtract(where, outers, [delta, delta_1, delta_2, delta_3])
    projected = place(where, pieces, widths)
    new_moment = jnp.concatenate(new_moments, axis=1)
    edge = widths[0] + widths[1]
    return (
        projected,
        *new_outers,
        new_moment[:, : widths[0]],
        new_moment[:, widths[0] : edge],
        new_moment[:, edge:],
    )


def solution(mesh):
    placed = (
        P(("replica", "fsdp"), None),
        P("replica", "fsdp", None),
        P("replica", "fsdp", None),
        P("replica", "fsdp", None),
        P("fsdp", None),
        P("fsdp", None),
        P("fsdp", None),
        P("fsdp", "replica"),
        P("fsdp", "replica"),
        P("fsdp", "replica"),
    )
    return jax.shard_map(
        per_device,
        mesh=mesh,
        in_specs=placed,
        out_specs=(
            P(("replica", "fsdp"), None),
            P("fsdp", None),
            P("fsdp", None),
            P("fsdp", None),
            P("fsdp", "replica"),
            P("fsdp", "replica"),
            P("fsdp", "replica"),
        ),
        check_vma=False,
    )
```

```python
import functools

import jax
import jax.numpy as jnp
from jax import lax
from jax.experimental import pallas as pl
from jax.experimental.pallas import tpu as pltpu
from jax.sharding import PartitionSpec as P

LEARN_RATE = 0.7
MOMENTUM_BETA = 0.9
SMALL_VMEM = 20 * 1024 * 1024
SHORTEST_RING = 8
LONGEST_RING = 16


def from_replica(x, distance):
    count = lax.axis_size("replica")
    return lax.ppermute(x, "replica", [(i, i ^ distance) for i in range(count)])


def ring_member(p, n):
    return 2 * p if p < n // 2 else 2 * (n - 1 - p) + 1


def source_of(row, steps, n):
    p = jnp.where(row % 2 == 0, row // 2, n - 1 - row // 2)
    p = (p - steps + n) % n
    return jnp.where(p < n // 2, 2 * p, 2 * (n - 1 - p) + 1)


def after(x, *others):
    return lax.optimization_barrier((x, *others))[0]


def fetch(sources, buffers, sems):
    copies = [pltpu.make_async_copy(a, b, sems.at[i]) for i, (a, b) in enumerate(zip(sources, buffers))]
    for copy in copies:
        copy.start()
    for copy in copies:
        copy.wait()


def columns_at(ref, block, width):
    return ref.at[:, pl.ds(pl.multiple_of(block * width, width), width)]


def in_hbm(arrays):
    return [pltpu.with_memory_space_constraint(a, pltpu.HBM) for a in arrays]


def spread(pieces, outs):
    edges = [0]
    for piece in pieces:
        edges.append(edges[-1] + piece.shape[1])
    left = 0
    for out in outs:
        right = left + out.shape[1]
        for piece, start in zip(pieces, edges):
            low, high = max(left, start), min(right, start + piece.shape[1])
            if low < high:
                out[:, low - left : high - left] = piece[:, low - start : high - start].astype(out.dtype)
        left = right


def columns_call(kernel, name, where, arrays, shapes, buffers):
    return pl.pallas_call(
        kernel,
        out_shape=shapes,
        in_specs=[pl.BlockSpec(memory_space=pltpu.SMEM)] + [pl.BlockSpec(memory_space=pl.ANY)] * len(arrays),
        out_specs=[pl.BlockSpec(memory_space=pltpu.VMEM)] * len(shapes),
        scratch_shapes=[*buffers, pltpu.SemaphoreType.DMA((len(arrays) * 2,))],
        compiler_params=pltpu.CompilerParams(vmem_limit_bytes=SMALL_VMEM),
        name=name,
    )(where, *in_hbm(arrays))


def pack_kernel(widths, distances, where, *refs):
    sources, outs, sems = refs[: len(widths)], refs[len(widths) : -1], refs[-1]
    views, targets = [], []
    for distance, out in zip(distances, outs):
        left = 0
        for source, width in zip(sources, widths):
            views.append(columns_at(source, lax.bitwise_xor(where[0], distance), width))
            targets.append(out.at[:, pl.ds(left, width)])
            left += width
    fetch(views, targets, sems)


def pack(where, arrays, widths, distances, name):
    shapes = [jax.ShapeDtypeStruct((arrays[0].shape[0], sum(widths)), arrays[0].dtype) for _ in distances]
    kernel = functools.partial(pack_kernel, widths, distances)
    return columns_call(kernel, name, where, arrays, shapes, [])


def half_kernel(distance, where, *refs):
    sources, outs, buffers, sems = refs[:6], refs[6:-7], refs[-7:-1], refs[-1]
    block = lax.bitwise_xor(where[0], distance)
    fetch([columns_at(r, block, b.shape[1]) for r, b in zip(sources, buffers)], buffers, sems)
    left = 0
    for inner, outer in zip(buffers[:3], buffers[3:]):
        columns = pl.ds(left, outer.shape[1])
        base = outer[...]
        outs[0][:, columns] = base - inner[...].astype(jnp.float32)
        outs[1][:, columns] = base
        left += outer.shape[1]


def own_kernel(count, half, outer, sibling, remote, moment_q, moment_k, moment_v, *outs):
    delta, new_moments = outs[0], outs[1:]
    left = 0
    for moment, new in zip((moment_q, moment_k, moment_v), new_moments):
        columns = pl.ds(left, moment.shape[1])
        own = half[:, columns] + (outer[:, columns] - sibling[:, columns].astype(jnp.float32))
        pseudo = (own + remote[:, columns].astype(jnp.float32)) / count
        new_moment = MOMENTUM_BETA * moment[...] + pseudo
        step = LEARN_RATE * (pseudo + MOMENTUM_BETA * new_moment)
        new[...] = new_moment
        delta[:, columns] = step.astype(jnp.bfloat16)
        left += moment.shape[1]


def own_step(half, outer, sibling, remote, moments, count):
    shapes = [jax.ShapeDtypeStruct(half.shape, jnp.bfloat16)]
    shapes += [jax.ShapeDtypeStruct(m.shape, jnp.float32) for m in moments]
    return pl.pallas_call(
        functools.partial(own_kernel, count),
        out_shape=shapes,
        in_specs=[pl.BlockSpec(memory_space=pltpu.VMEM)] * 7,
        out_specs=[pl.BlockSpec(memory_space=pltpu.VMEM)] * len(shapes),
        compiler_params=pltpu.CompilerParams(vmem_limit_bytes=SMALL_VMEM),
        name="own_step",
    )(half, outer, sibling, remote, *moments)


def fresh_kernel(count, first, half, outer, sibling, remote, moment_q, moment_k, moment_v, out):
    left, last = 0, first + out.shape[1]
    for moment in (moment_q, moment_k, moment_v):
        low, high = max(left, first), min(left + moment.shape[1], last)
        if low < high:
            columns = pl.ds(low, high - low)
            own = half[:, columns] + (outer[:, columns] - sibling[:, columns].astype(jnp.float32))
            pseudo = (own + remote[:, low - first : high - first].astype(jnp.float32)) / count
            new_moment = MOMENTUM_BETA * moment[:, low - left : high - left] + pseudo
            step = LEARN_RATE * (pseudo + MOMENTUM_BETA * new_moment)
            out[:, low - first : high - first] = (outer[:, columns] - step).astype(jnp.bfloat16)
        left += moment.shape[1]


def fresh_columns(half, outer, sibling, remote, moments, first, count):
    return pl.pallas_call(
        functools.partial(fresh_kernel, count, first),
        out_shape=jax.ShapeDtypeStruct(remote.shape, jnp.bfloat16),
        in_specs=[pl.BlockSpec(memory_space=pltpu.VMEM)] * 7,
        out_specs=pl.BlockSpec(memory_space=pltpu.VMEM),
        compiler_params=pltpu.CompilerParams(vmem_limit_bytes=SMALL_VMEM),
        name="fresh_columns",
    )(half, outer, sibling, remote, *moments)


def subtract_kernel(where, outer_q, outer_k, outer_v, own, remote, pair, *outs):
    outers = (outer_q, outer_k, outer_v)
    width = own.shape[1]
    deltas = (own, pair.at[:, pl.ds(0, width)], remote, pair.at[:, pl.ds(width, width)])
    for distance, delta in enumerate(deltas):
        block = lax.bitwise_xor(where[0], distance)
        start = 0
        for outer, out in zip(outers, outs):
            width = outer.shape[1] // len(deltas)
            columns = pl.ds(pl.multiple_of(block * width, width), width)
            out[:, columns] = outer[:, columns] - delta[:, start : start + width].astype(jnp.float32)
            start += width


def subtract(where, outers, own, remote, pair):
    return pl.pallas_call(
        subtract_kernel,
        out_shape=[jax.ShapeDtypeStruct(o.shape, o.dtype) for o in outers],
        in_specs=[pl.BlockSpec(memory_space=pltpu.SMEM)] + [pl.BlockSpec(memory_space=pltpu.VMEM)] * 6,
        out_specs=[pl.BlockSpec(memory_space=pltpu.VMEM)] * len(outers),
        compiler_params=pltpu.CompilerParams(vmem_limit_bytes=SMALL_VMEM),
        name="outer_minus_delta",
    )(where, *outers, own, remote, pair)


def place_kernel(count, pieces, where, *refs):
    sources, out, sems = refs[:count], refs[-2], refs[-1]
    copies = []
    for distance, source in enumerate(sources):
        block = lax.bitwise_xor(where[0], distance)
        left = 0
        for start, stride, width in pieces:
            at = pl.multiple_of(start + block * stride, 128)
            copies.append((source.at[:, pl.ds(left, width)], out.at[:, pl.ds(at, width)]))
            left += width
    fetch([a for a, _ in copies], [b for _, b in copies], sems)


def place(where, sources, pieces, columns, earlier, name):
    held = [] if earlier is None else [earlier]
    return pl.pallas_call(
        functools.partial(place_kernel, len(sources), pieces),
        out_shape=jax.ShapeDtypeStruct((sources[0].shape[0], columns), jnp.bfloat16),
        in_specs=[pl.BlockSpec(memory_space=pltpu.SMEM)]
        + [pl.BlockSpec(memory_space=pltpu.VMEM)] * len(sources)
        + [pl.BlockSpec(memory_space=pl.ANY)] * len(held),
        out_specs=pl.BlockSpec(memory_space=pl.ANY),
        scratch_shapes=[pltpu.SemaphoreType.DMA((len(sources) * len(pieces),))],
        input_output_aliases={1 + len(sources): 0} if held else {},
        compiler_params=pltpu.CompilerParams(vmem_limit_bytes=SMALL_VMEM),
        name=name,
    )(where, *sources, *held)


def per_device(
    tokens, inner_q, inner_k, inner_v, outer_q, outer_k, outer_v, moment_q, moment_k, value_momentum
):
    count = lax.axis_size("replica")
    n = lax.axis_size("fsdp")
    me = lax.axis_index("replica")
    row = lax.axis_index("fsdp")
    inners = (inner_q[0], inner_k[0], inner_v[0])
    outers = (outer_q, outer_k, outer_v)
    moments = (moment_q, moment_k, value_momentum)
    widths = [m.shape[1] for m in moments]
    rows = outer_q.shape[0]
    mine = tokens.shape[0]
    total_width = sum(widths)
    cut = total_width // 2
    streams = (cut, total_width - cut)
    LAG, LEAD = 0, 1

    where = me.astype(jnp.int32).reshape(1)
    block = jax.ShapeDtypeStruct((rows, total_width), jnp.float32)
    buffers = [pltpu.VMEM((rows, w), a.dtype) for a, w in zip((*inners, *outers), widths * 2)]

    def half(distance, name, where):
        kernel = functools.partial(half_kernel, distance)
        return columns_call(kernel, name, where, (*inners, *outers), [block] * 2, buffers)

    far_pack, near_pack = pack(where, inners, widths, (3, 1), "pack_inner")
    far_sibling = from_replica(far_pack, 1)
    near_sibling = from_replica(near_pack, 1)
    far_half, far_outer = half(2, "far_half", where)
    far = far_half + (far_outer - far_sibling.astype(jnp.float32))
    fars = [far[:, :cut].astype(jnp.bfloat16), far[:, cut:].astype(jnp.bfloat16)]
    remotes = [from_replica(f, 2) for f in fars]
    near_half, own_outer = half(0, "near_half", after(where, fars[LEAD]))

    tokens_1 = from_replica(after(tokens, fars[LEAD]), 1)
    near_tokens = jnp.concatenate([tokens, tokens_1], axis=0)
    parts = (near_half, own_outer, near_sibling)
    fresh = [
        fresh_columns(*parts, after(remotes[LAG], near_tokens), moments, 0, count),
        fresh_columns(*parts, remotes[LEAD], moments, cut, count),
    ]
    tokens_2 = from_replica(after(tokens, remotes[LEAD]), 2)

    def whole_step(*others):
        remote = jnp.concatenate([after(remotes[0], *others), remotes[1]], axis=1)
        return own_step(*parts, remote, moments, count)

    up = [(ring_member(p, n), ring_member((p + 1) % n, n)) for p in range(n)]
    down = [(b, a) for a, b in up]
    last = n // 2

    def product(lhs, steps, block):
        lanes = lax.dynamic_slice_in_dim(lhs, source_of(row, steps, n) * rows, rows, 1)
        return jnp.dot(lanes, block, preferred_element_type=jnp.float32)

    if n % 2 or not SHORTEST_RING <= n <= LONGEST_RING:
        gathered = [lax.all_gather(part, "fsdp", axis=0, tiled=True) for part in fresh]
        tokens_3 = from_replica(tokens_2, 1)
        far_tokens = jnp.concatenate([tokens_2, tokens_3], axis=0)
        delta, *new_moments = whole_step()
        delta_2 = from_replica(delta, 2)
        near_totals = [jnp.dot(near_tokens, g, preferred_element_type=jnp.float32) for g in gathered]
        far_totals = [jnp.dot(far_tokens, g, preferred_element_type=jnp.float32) for g in gathered]
    else:
        heads = [[part, part] for part in fresh]
        arrived = [[(0, part)] for part in fresh]
        near_totals = [product(near_tokens, 0, part) for part in fresh]
        far_totals = [None, None]

        def hop(stream, way, step, *others):
            heads[stream][way] = lax.ppermute(after(heads[stream][way], *others), "fsdp", (up, down)[way])
            arrived[stream].append((step if way == 0 else -step, heads[stream][way]))

        def add_near(stream, blocks):
            for block in blocks:
                near_totals[stream] += product(near_tokens, *block)

        def add_far(stream, blocks, *others):
            for steps, block in blocks:
                value = product(far_tokens, steps, after(block, *others) if others else block)
                far_totals[stream] = value if far_totals[stream] is None else far_totals[stream] + value

        def hold(stream, first, *others):
            arrived[stream][first:] = [(steps, after(block, *others)) for steps, block in arrived[stream][first:]]

        hop(LEAD, 0, 1)
        hop(LEAD, 1, 1)
        heads[LAG] = [after(block, *heads[LEAD]) for block in heads[LAG]]
        hop(LAG, 0, 1, near_totals[LAG])
        hop(LAG, 1, 1, near_totals[LAG])
        add_near(LEAD, arrived[LEAD][-2:])
        add_near(LAG, arrived[LAG][-2:])
        delta, *new_moments = whole_step(near_totals[LEAD])
        for step in range(2, last):
            for stream in (LEAD, LAG):
                hop(stream, 0, step, near_totals[stream])
                hop(stream, 1, step, near_totals[stream])
            if step < last - 1:
                add_near(LEAD, arrived[LEAD][-2:])
                add_near(LAG, arrived[LAG][-2:])
            if step == 2:
                tokens_2 = after(tokens_2, heads[LAG][0])
                tokens_3 = from_replica(tokens_2, 1)
                far_tokens = jnp.concatenate([tokens_2, tokens_3], axis=0)
                delta_2 = from_replica(after(delta, tokens_2), 2)
        add_near(LEAD, arrived[LEAD][-2:])
        hop(LEAD, 0, last, near_totals[LEAD])
        add_far(LEAD, arrived[LEAD][:-1])
        hold(LAG, -2, far_totals[LEAD])
        add_near(LAG, arrived[LAG][-2:])
        hop(LAG, 1, last, near_totals[LAG])
        hold(LEAD, -1, near_totals[LAG])
        add_near(LEAD, arrived[LEAD][-1:])
        add_far(LEAD, arrived[LEAD][-1:])
        hold(LAG, -1, near_totals[LEAD], delta_2)
        add_near(LAG, arrived[LAG][-1:])
        add_far(LAG, arrived[LAG], near_totals[LAG])

    held = [after(d, near_totals[LAG]) for d in (delta, delta_2)]
    pair = from_replica(jnp.concatenate(held, axis=1), 1)
    new_outers = subtract(where, outers, delta, delta_2, pair)

    base_k, base_v = count * widths[0], count * (widths[0] + widths[1])
    pieces = (
        ((0, widths[0], cut),),
        ((cut, widths[0], widths[0] - cut), (base_k, widths[1], widths[1]), (base_v, widths[2], widths[2])),
    )
    projected = None
    for stream, name in ((LEAD, "place_leading"), (LAG, "place_second")):
        near_out = near_totals[stream].astype(jnp.bfloat16)
        far_out = far_totals[stream].astype(jnp.bfloat16)
        sources = [
            near_out[:mine],
            from_replica(near_out[mine:], 1),
            from_replica(far_out[:mine], 2),
            from_replica(far_out[mine:], 3),
        ]
        if projected is not None:
            projected = after(projected, *new_outers)
        projected = place(where, sources, pieces[stream], count * total_width, projected, name)
    return projected, *new_outers, *new_moments


def solution(mesh):
    placed = (
        P(("replica", "fsdp"), None),
        P("replica", "fsdp", None),
        P("replica", "fsdp", None),
        P("replica", "fsdp", None),
        P("fsdp", None),
        P("fsdp", None),
        P("fsdp", None),
        P("fsdp", "replica"),
        P("fsdp", "replica"),
        P("fsdp", "replica"),
    )
    return jax.shard_map(
        per_device,
        mesh=mesh,
        in_specs=placed,
        out_specs=(
            P(("replica", "fsdp"), None),
            P("fsdp", None),
            P("fsdp", None),
            P("fsdp", None),
            P("fsdp", "replica"),
            P("fsdp", "replica"),
            P("fsdp", "replica"),
        ),
        check_vma=False,
    )
```

```python
import functools

import jax
import jax.numpy as jnp
from jax import lax
from jax.experimental import pallas as pl
from jax.experimental.pallas import tpu as pltpu
from jax.sharding import PartitionSpec as P

LEARN_RATE = 0.7
MOMENTUM_BETA = 0.9
SMALL_VMEM = 20 * 1024 * 1024
SHORTEST_RING = 8
LONGEST_RING = 16


def from_replica(x, distance):
    count = lax.axis_size("replica")
    return lax.ppermute(x, "replica", [(i, i ^ distance) for i in range(count)])


def ring_member(p, n):
    return 2 * p if p < n // 2 else 2 * (n - 1 - p) + 1


def source_of(row, steps, n):
    p = jnp.where(row % 2 == 0, row // 2, n - 1 - row // 2)
    p = (p - steps + n) % n
    return jnp.where(p < n // 2, 2 * p, 2 * (n - 1 - p) + 1)


def after(x, *others):
    return lax.optimization_barrier((x, *others))[0]


def fetch(sources, buffers, sems):
    copies = [pltpu.make_async_copy(a, b, sems.at[i]) for i, (a, b) in enumerate(zip(sources, buffers))]
    for copy in copies:
        copy.start()
    for copy in copies:
        copy.wait()


def columns_at(ref, block, width):
    return ref.at[:, pl.ds(pl.multiple_of(block * width, width), width)]


def in_hbm(arrays):
    return [pltpu.with_memory_space_constraint(a, pltpu.HBM) for a in arrays]


def spread(pieces, outs):
    edges = [0]
    for piece in pieces:
        edges.append(edges[-1] + piece.shape[1])
    left = 0
    for out in outs:
        right = left + out.shape[1]
        for piece, start in zip(pieces, edges):
            low, high = max(left, start), min(right, start + piece.shape[1])
            if low < high:
                out[:, low - left : high - left] = piece[:, low - start : high - start].astype(out.dtype)
        left = right


def columns_call(kernel, name, where, arrays, shapes, buffers):
    return pl.pallas_call(
        kernel,
        out_shape=shapes,
        in_specs=[pl.BlockSpec(memory_space=pltpu.SMEM)] + [pl.BlockSpec(memory_space=pl.ANY)] * len(arrays),
        out_specs=[pl.BlockSpec(memory_space=pltpu.VMEM)] * len(shapes),
        scratch_shapes=[*buffers, pltpu.SemaphoreType.DMA((len(arrays) * 2,))],
        compiler_params=pltpu.CompilerParams(vmem_limit_bytes=SMALL_VMEM),
        name=name,
    )(where, *in_hbm(arrays))


def pack_kernel(widths, distances, where, *refs):
    sources, outs, sems = refs[: len(widths)], refs[len(widths) : -1], refs[-1]
    views, targets = [], []
    for distance, out in zip(distances, outs):
        left = 0
        for source, width in zip(sources, widths):
            views.append(columns_at(source, lax.bitwise_xor(where[0], distance), width))
            targets.append(out.at[:, pl.ds(left, width)])
            left += width
    fetch(views, targets, sems)


def pack(where, arrays, widths, distances, name):
    shapes = [jax.ShapeDtypeStruct((arrays[0].shape[0], sum(widths)), arrays[0].dtype) for _ in distances]
    kernel = functools.partial(pack_kernel, widths, distances)
    return columns_call(kernel, name, where, arrays, shapes, [])


def half_kernel(distance, where, *refs):
    sources, outs, buffers, sems = refs[:6], refs[6:-7], refs[-7:-1], refs[-1]
    block = lax.bitwise_xor(where[0], distance)
    fetch([columns_at(r, block, b.shape[1]) for r, b in zip(sources, buffers)], buffers, sems)
    left = 0
    for inner, outer in zip(buffers[:3], buffers[3:]):
        columns = pl.ds(left, outer.shape[1])
        base = outer[...]
        outs[0][:, columns] = base - inner[...].astype(jnp.float32)
        outs[1][:, columns] = base
        left += outer.shape[1]


def own_kernel(count, half, outer, sibling, remote, moment_q, moment_k, moment_v, *outs):
    delta, new_moments = outs[0], outs[1:]
    left = 0
    for moment, new in zip((moment_q, moment_k, moment_v), new_moments):
        columns = pl.ds(left, moment.shape[1])
        own = half[:, columns] + (outer[:, columns] - sibling[:, columns].astype(jnp.float32))
        pseudo = (own + remote[:, columns].astype(jnp.float32)) / count
        new_moment = MOMENTUM_BETA * moment[...] + pseudo
        step = LEARN_RATE * (pseudo + MOMENTUM_BETA * new_moment)
        new[...] = new_moment
        delta[:, columns] = step.astype(jnp.bfloat16)
        left += moment.shape[1]


def own_step(half, outer, sibling, remote, moments, count):
    shapes = [jax.ShapeDtypeStruct(half.shape, jnp.bfloat16)]
    shapes += [jax.ShapeDtypeStruct(m.shape, jnp.float32) for m in moments]
    return pl.pallas_call(
        functools.partial(own_kernel, count),
        out_shape=shapes,
        in_specs=[pl.BlockSpec(memory_space=pltpu.VMEM)] * 7,
        out_specs=[pl.BlockSpec(memory_space=pltpu.VMEM)] * len(shapes),
        compiler_params=pltpu.CompilerParams(vmem_limit_bytes=SMALL_VMEM),
        name="own_step",
    )(half, outer, sibling, remote, *moments)


def fresh_kernel(count, first, half, outer, sibling, remote, moment_q, moment_k, moment_v, out):
    left, last = 0, first + out.shape[1]
    for moment in (moment_q, moment_k, moment_v):
        low, high = max(left, first), min(left + moment.shape[1], last)
        if low < high:
            columns = pl.ds(low, high - low)
            own = half[:, columns] + (outer[:, columns] - sibling[:, columns].astype(jnp.float32))
            pseudo = (own + remote[:, low - first : high - first].astype(jnp.float32)) / count
            new_moment = MOMENTUM_BETA * moment[:, low - left : high - left] + pseudo
            step = LEARN_RATE * (pseudo + MOMENTUM_BETA * new_moment)
            out[:, low - first : high - first] = (outer[:, columns] - step).astype(jnp.bfloat16)
        left += moment.shape[1]


def fresh_columns(half, outer, sibling, remote, moments, first, count):
    return pl.pallas_call(
        functools.partial(fresh_kernel, count, first),
        out_shape=jax.ShapeDtypeStruct(remote.shape, jnp.bfloat16),
        in_specs=[pl.BlockSpec(memory_space=pltpu.VMEM)] * 7,
        out_specs=pl.BlockSpec(memory_space=pltpu.VMEM),
        compiler_params=pltpu.CompilerParams(vmem_limit_bytes=SMALL_VMEM),
        name="fresh_columns",
    )(half, outer, sibling, remote, *moments)


def subtract_kernel(where, outer_q, outer_k, outer_v, own, remote, pair, *outs):
    outers = (outer_q, outer_k, outer_v)
    width = own.shape[1]
    deltas = (own, pair.at[:, pl.ds(0, width)], remote, pair.at[:, pl.ds(width, width)])
    for distance, delta in enumerate(deltas):
        block = lax.bitwise_xor(where[0], distance)
        start = 0
        for outer, out in zip(outers, outs):
            width = outer.shape[1] // len(deltas)
            columns = pl.ds(pl.multiple_of(block * width, width), width)
            out[:, columns] = outer[:, columns] - delta[:, start : start + width].astype(jnp.float32)
            start += width


def subtract(where, outers, own, remote, pair):
    return pl.pallas_call(
        subtract_kernel,
        out_shape=[jax.ShapeDtypeStruct(o.shape, o.dtype) for o in outers],
        in_specs=[pl.BlockSpec(memory_space=pltpu.SMEM)] + [pl.BlockSpec(memory_space=pltpu.VMEM)] * 6,
        out_specs=[pl.BlockSpec(memory_space=pltpu.VMEM)] * len(outers),
        compiler_params=pltpu.CompilerParams(vmem_limit_bytes=SMALL_VMEM),
        name="outer_minus_delta",
    )(where, *outers, own, remote, pair)


def place_kernel(count, pieces, where, *refs):
    sources, out, sems = refs[:count], refs[-2], refs[-1]
    copies = []
    for distance, source in enumerate(sources):
        block = lax.bitwise_xor(where[0], distance)
        left = 0
        for start, stride, width in pieces:
            at = pl.multiple_of(start + block * stride, 128)
            copies.append((source.at[:, pl.ds(left, width)], out.at[:, pl.ds(at, width)]))
            left += width
    fetch([a for a, _ in copies], [b for _, b in copies], sems)


def place(where, sources, pieces, columns, earlier, name):
    held = [] if earlier is None else [earlier]
    return pl.pallas_call(
        functools.partial(place_kernel, len(sources), pieces),
        out_shape=jax.ShapeDtypeStruct((sources[0].shape[0], columns), jnp.bfloat16),
        in_specs=[pl.BlockSpec(memory_space=pltpu.SMEM)]
        + [pl.BlockSpec(memory_space=pltpu.VMEM)] * len(sources)
        + [pl.BlockSpec(memory_space=pl.ANY)] * len(held),
        out_specs=pl.BlockSpec(memory_space=pl.ANY),
        scratch_shapes=[pltpu.SemaphoreType.DMA((len(sources) * len(pieces),))],
        input_output_aliases={1 + len(sources): 0} if held else {},
        compiler_params=pltpu.CompilerParams(vmem_limit_bytes=SMALL_VMEM),
        name=name,
    )(where, *sources, *held)


def per_device(
    tokens, inner_q, inner_k, inner_v, outer_q, outer_k, outer_v, moment_q, moment_k, value_momentum
):
    count = lax.axis_size("replica")
    n = lax.axis_size("fsdp")
    me = lax.axis_index("replica")
    row = lax.axis_index("fsdp")
    inners = (inner_q[0], inner_k[0], inner_v[0])
    outers = (outer_q, outer_k, outer_v)
    moments = (moment_q, moment_k, value_momentum)
    widths = [m.shape[1] for m in moments]
    rows = outer_q.shape[0]
    mine = tokens.shape[0]
    total_width = sum(widths)
    cut = total_width // 2
    streams = (cut, total_width - cut)
    LAG, LEAD = 0, 1

    where = me.astype(jnp.int32).reshape(1)
    block = jax.ShapeDtypeStruct((rows, total_width), jnp.float32)
    buffers = [pltpu.VMEM((rows, w), a.dtype) for a, w in zip((*inners, *outers), widths * 2)]

    def half(distance, name, where):
        kernel = functools.partial(half_kernel, distance)
        return columns_call(kernel, name, where, (*inners, *outers), [block] * 2, buffers)

    far_pack, near_pack = pack(where, inners, widths, (3, 1), "pack_inner")
    far_sibling = from_replica(far_pack, 1)
    near_sibling = from_replica(near_pack, 1)
    far_half, far_outer = half(2, "far_half", where)
    far = far_half + (far_outer - far_sibling.astype(jnp.float32))
    fars = [far[:, :cut].astype(jnp.bfloat16), far[:, cut:].astype(jnp.bfloat16)]
    remotes = [from_replica(f, 2) for f in fars]
    near_half, own_outer = half(0, "near_half", after(where, fars[LEAD]))

    tokens_1 = from_replica(tokens, 1)
    near_tokens = jnp.concatenate([tokens, tokens_1], axis=0)
    parts = (near_half, own_outer, near_sibling)
    fresh = [
        fresh_columns(*parts, after(remotes[LAG], near_tokens), moments, 0, count),
        fresh_columns(*parts, remotes[LEAD], moments, cut, count),
    ]
    tokens_2 = from_replica(after(tokens, remotes[LEAD]), 2)

    def whole_step(*others):
        remote = jnp.concatenate([after(remotes[0], *others), remotes[1]], axis=1)
        return own_step(*parts, remote, moments, count)

    up = [(ring_member(p, n), ring_member((p + 1) % n, n)) for p in range(n)]
    down = [(b, a) for a, b in up]
    last = n // 2

    def product(lhs, steps, block):
        lanes = lax.dynamic_slice_in_dim(lhs, source_of(row, steps, n) * rows, rows, 1)
        return jnp.dot(lanes, block, preferred_element_type=jnp.float32)

    if n % 2 or not SHORTEST_RING <= n <= LONGEST_RING:
        gathered = [lax.all_gather(part, "fsdp", axis=0, tiled=True) for part in fresh]
        tokens_3 = from_replica(tokens_2, 1)
        far_tokens = jnp.concatenate([tokens_2, tokens_3], axis=0)
        delta, *new_moments = whole_step()
        delta_2 = from_replica(delta, 2)
        near_totals = [jnp.dot(near_tokens, g, preferred_element_type=jnp.float32) for g in gathered]
        far_totals = [jnp.dot(far_tokens, g, preferred_element_type=jnp.float32) for g in gathered]
    else:
        heads = [[part, part] for part in fresh]
        arrived = [[(0, part)] for part in fresh]
        near_totals = [product(near_tokens, 0, part) for part in fresh]
        far_totals = [None, None]

        def hop(stream, way, step, *others):
            heads[stream][way] = lax.ppermute(after(heads[stream][way], *others), "fsdp", (up, down)[way])
            arrived[stream].append((step if way == 0 else -step, heads[stream][way]))

        def add_near(stream, blocks):
            for block in blocks:
                near_totals[stream] += product(near_tokens, *block)

        def add_far(stream, blocks, *others):
            for steps, block in blocks:
                value = product(far_tokens, steps, after(block, *others) if others else block)
                far_totals[stream] = value if far_totals[stream] is None else far_totals[stream] + value

        def hold(stream, first, *others):
            arrived[stream][first:] = [(steps, after(block, *others)) for steps, block in arrived[stream][first:]]

        hop(LEAD, 0, 1)
        hop(LEAD, 1, 1)
        heads[LAG] = [after(block, *heads[LEAD]) for block in heads[LAG]]
        hop(LAG, 0, 1, near_totals[LAG])
        hop(LAG, 1, 1, near_totals[LAG])
        add_near(LEAD, arrived[LEAD][-2:])
        add_near(LAG, arrived[LAG][-2:])
        delta, *new_moments = whole_step(near_totals[LEAD])
        for step in range(2, last):
            for stream in (LEAD, LAG):
                hop(stream, 0, step, near_totals[stream])
                hop(stream, 1, step, near_totals[stream])
            if step < last - 1:
                add_near(LEAD, arrived[LEAD][-2:])
                add_near(LAG, arrived[LAG][-2:])
            if step == 2:
                tokens_2 = after(tokens_2, heads[LAG][0])
                tokens_3 = from_replica(tokens_2, 1)
                far_tokens = jnp.concatenate([tokens_2, tokens_3], axis=0)
                delta_2 = from_replica(after(delta, tokens_2), 2)
        add_near(LEAD, arrived[LEAD][-2:])
        hop(LEAD, 0, last, near_totals[LEAD])
        add_far(LEAD, arrived[LEAD][:-1])
        hold(LAG, -2, far_totals[LEAD])
        add_near(LAG, arrived[LAG][-2:])
        hop(LAG, 1, last, near_totals[LAG])
        hold(LEAD, -1, near_totals[LAG])
        add_near(LEAD, arrived[LEAD][-1:])
        add_far(LEAD, arrived[LEAD][-1:])
        hold(LAG, -1, near_totals[LEAD], delta_2)
        add_far(LAG, arrived[LAG][:-1], near_totals[LEAD], far_totals[LEAD])
        add_near(LAG, arrived[LAG][-1:])
        add_far(LAG, arrived[LAG][-1:], near_totals[LAG])

    held = [after(d, near_totals[LAG]) for d in (delta, delta_2)]
    pair = from_replica(jnp.concatenate(held, axis=1), 1)
    new_outers = subtract(where, outers, delta, delta_2, pair)

    base_k, base_v = count * widths[0], count * (widths[0] + widths[1])
    pieces = (
        ((0, widths[0], cut),),
        ((cut, widths[0], widths[0] - cut), (base_k, widths[1], widths[1]), (base_v, widths[2], widths[2])),
    )
    projected = None
    for stream, name in ((LEAD, "place_leading"), (LAG, "place_second")):
        near_out = near_totals[stream].astype(jnp.bfloat16)
        far_out = far_totals[stream].astype(jnp.bfloat16)
        sources = [
            near_out[:mine],
            from_replica(near_out[mine:], 1),
            from_replica(far_out[:mine], 2),
            from_replica(far_out[mine:], 3),
        ]
        if projected is not None:
            projected = after(projected, *new_outers)
        projected = place(where, sources, pieces[stream], count * total_width, projected, name)
    return projected, *new_outers, *new_moments


def solution(mesh):
    placed = (
        P(("replica", "fsdp"), None),
        P("replica", "fsdp", None),
        P("replica", "fsdp", None),
        P("replica", "fsdp", None),
        P("fsdp", None),
        P("fsdp", None),
        P("fsdp", None),
        P("fsdp", "replica"),
        P("fsdp", "replica"),
        P("fsdp", "replica"),
    )
    return jax.shard_map(
        per_device,
        mesh=mesh,
        in_specs=placed,
        out_specs=(
            P(("replica", "fsdp"), None),
            P("fsdp", None),
            P("fsdp", None),
            P("fsdp", None),
            P("fsdp", "replica"),
            P("fsdp", "replica"),
            P("fsdp", "replica"),
        ),
        check_vma=False,
    )
```

```python
import functools

import jax
import jax.numpy as jnp
from jax import lax
from jax.experimental import pallas as pl
from jax.experimental.pallas import tpu as pltpu
from jax.sharding import PartitionSpec as P

LEARN_RATE = 0.7
MOMENTUM_BETA = 0.9
SMALL_VMEM = 20 * 1024 * 1024
SHORTEST_RING = 8
LONGEST_RING = 16


def from_replica(x, distance):
    count = lax.axis_size("replica")
    return lax.ppermute(x, "replica", [(i, i ^ distance) for i in range(count)])


def ring_member(p, n):
    return 2 * p if p < n // 2 else 2 * (n - 1 - p) + 1


def source_of(row, steps, n):
    p = jnp.where(row % 2 == 0, row // 2, n - 1 - row // 2)
    p = (p - steps + n) % n
    return jnp.where(p < n // 2, 2 * p, 2 * (n - 1 - p) + 1)


def after(x, *others):
    return lax.optimization_barrier((x, *others))[0]


def fetch(sources, buffers, sems):
    copies = [pltpu.make_async_copy(a, b, sems.at[i]) for i, (a, b) in enumerate(zip(sources, buffers))]
    for copy in copies:
        copy.start()
    for copy in copies:
        copy.wait()


def columns_at(ref, block, width):
    return ref.at[:, pl.ds(pl.multiple_of(block * width, width), width)]


def in_hbm(arrays):
    return [pltpu.with_memory_space_constraint(a, pltpu.HBM) for a in arrays]


def spread(pieces, outs):
    edges = [0]
    for piece in pieces:
        edges.append(edges[-1] + piece.shape[1])
    left = 0
    for out in outs:
        right = left + out.shape[1]
        for piece, start in zip(pieces, edges):
            low, high = max(left, start), min(right, start + piece.shape[1])
            if low < high:
                out[:, low - left : high - left] = piece[:, low - start : high - start].astype(out.dtype)
        left = right


def columns_call(kernel, name, where, arrays, shapes, buffers):
    return pl.pallas_call(
        kernel,
        out_shape=shapes,
        in_specs=[pl.BlockSpec(memory_space=pltpu.SMEM)] + [pl.BlockSpec(memory_space=pl.ANY)] * len(arrays),
        out_specs=[pl.BlockSpec(memory_space=pltpu.VMEM)] * len(shapes),
        scratch_shapes=[*buffers, pltpu.SemaphoreType.DMA((len(arrays) * 2,))],
        compiler_params=pltpu.CompilerParams(vmem_limit_bytes=SMALL_VMEM),
        name=name,
    )(where, *in_hbm(arrays))


def pack_kernel(widths, distances, where, *refs):
    sources, outs, sems = refs[: len(widths)], refs[len(widths) : -1], refs[-1]
    views, targets = [], []
    for distance, out in zip(distances, outs):
        left = 0
        for source, width in zip(sources, widths):
            views.append(columns_at(source, lax.bitwise_xor(where[0], distance), width))
            targets.append(out.at[:, pl.ds(left, width)])
            left += width
    fetch(views, targets, sems)


def pack(where, arrays, widths, distances, name):
    shapes = [jax.ShapeDtypeStruct((arrays[0].shape[0], sum(widths)), arrays[0].dtype) for _ in distances]
    kernel = functools.partial(pack_kernel, widths, distances)
    return columns_call(kernel, name, where, arrays, shapes, [])


def half_kernel(distance, where, *refs):
    sources, outs, buffers, sems = refs[:6], refs[6:-7], refs[-7:-1], refs[-1]
    block = lax.bitwise_xor(where[0], distance)
    fetch([columns_at(r, block, b.shape[1]) for r, b in zip(sources, buffers)], buffers, sems)
    left = 0
    for inner, outer in zip(buffers[:3], buffers[3:]):
        columns = pl.ds(left, outer.shape[1])
        base = outer[...]
        outs[0][:, columns] = base - inner[...].astype(jnp.float32)
        outs[1][:, columns] = base
        left += outer.shape[1]


def own_kernel(count, half, outer, sibling, remote, moment_q, moment_k, moment_v, *outs):
    delta, new_moments = outs[0], outs[1:]
    left = 0
    for moment, new in zip((moment_q, moment_k, moment_v), new_moments):
        columns = pl.ds(left, moment.shape[1])
        own = half[:, columns] + (outer[:, columns] - sibling[:, columns].astype(jnp.float32))
        pseudo = (own + remote[:, columns].astype(jnp.float32)) / count
        new_moment = MOMENTUM_BETA * moment[...] + pseudo
        step = LEARN_RATE * (pseudo + MOMENTUM_BETA * new_moment)
        new[...] = new_moment
        delta[:, columns] = step.astype(jnp.bfloat16)
        left += moment.shape[1]


def own_step(half, outer, sibling, remote, moments, count):
    shapes = [jax.ShapeDtypeStruct(half.shape, jnp.bfloat16)]
    shapes += [jax.ShapeDtypeStruct(m.shape, jnp.float32) for m in moments]
    return pl.pallas_call(
        functools.partial(own_kernel, count),
        out_shape=shapes,
        in_specs=[pl.BlockSpec(memory_space=pltpu.VMEM)] * 7,
        out_specs=[pl.BlockSpec(memory_space=pltpu.VMEM)] * len(shapes),
        compiler_params=pltpu.CompilerParams(vmem_limit_bytes=SMALL_VMEM),
        name="own_step",
    )(half, outer, sibling, remote, *moments)


def fresh_kernel(count, first, half, outer, sibling, remote, moment_q, moment_k, moment_v, out):
    left, last = 0, first + out.shape[1]
    for moment in (moment_q, moment_k, moment_v):
        low, high = max(left, first), min(left + moment.shape[1], last)
        if low < high:
            columns = pl.ds(low, high - low)
            own = half[:, columns] + (outer[:, columns] - sibling[:, columns].astype(jnp.float32))
            pseudo = (own + remote[:, low - first : high - first].astype(jnp.float32)) / count
            new_moment = MOMENTUM_BETA * moment[:, low - left : high - left] + pseudo
            step = LEARN_RATE * (pseudo + MOMENTUM_BETA * new_moment)
            out[:, low - first : high - first] = (outer[:, columns] - step).astype(jnp.bfloat16)
        left += moment.shape[1]


def fresh_columns(half, outer, sibling, remote, moments, first, count):
    return pl.pallas_call(
        functools.partial(fresh_kernel, count, first),
        out_shape=jax.ShapeDtypeStruct(remote.shape, jnp.bfloat16),
        in_specs=[pl.BlockSpec(memory_space=pltpu.VMEM)] * 7,
        out_specs=pl.BlockSpec(memory_space=pltpu.VMEM),
        compiler_params=pltpu.CompilerParams(vmem_limit_bytes=SMALL_VMEM),
        name="fresh_columns",
    )(half, outer, sibling, remote, *moments)


def subtract_kernel(where, outer_q, outer_k, outer_v, own, remote, pair, *outs):
    outers = (outer_q, outer_k, outer_v)
    width = own.shape[1]
    deltas = (own, pair.at[:, pl.ds(0, width)], remote, pair.at[:, pl.ds(width, width)])
    for distance, delta in enumerate(deltas):
        block = lax.bitwise_xor(where[0], distance)
        start = 0
        for outer, out in zip(outers, outs):
            width = outer.shape[1] // len(deltas)
            columns = pl.ds(pl.multiple_of(block * width, width), width)
            out[:, columns] = outer[:, columns] - delta[:, start : start + width].astype(jnp.float32)
            start += width


def subtract(where, outers, own, remote, pair):
    return pl.pallas_call(
        subtract_kernel,
        out_shape=[jax.ShapeDtypeStruct(o.shape, o.dtype) for o in outers],
        in_specs=[pl.BlockSpec(memory_space=pltpu.SMEM)] + [pl.BlockSpec(memory_space=pltpu.VMEM)] * 6,
        out_specs=[pl.BlockSpec(memory_space=pltpu.VMEM)] * len(outers),
        compiler_params=pltpu.CompilerParams(vmem_limit_bytes=SMALL_VMEM),
        name="outer_minus_delta",
    )(where, *outers, own, remote, pair)


def place_kernel(count, pieces, where, *refs):
    sources, out, sems = refs[:count], refs[-2], refs[-1]
    copies = []
    for distance, source in enumerate(sources):
        block = lax.bitwise_xor(where[0], distance)
        left = 0
        for start, stride, width in pieces:
            at = pl.multiple_of(start + block * stride, 128)
            copies.append((source.at[:, pl.ds(left, width)], out.at[:, pl.ds(at, width)]))
            left += width
    fetch([a for a, _ in copies], [b for _, b in copies], sems)


def place(where, sources, pieces, columns, earlier, name):
    held = [] if earlier is None else [earlier]
    return pl.pallas_call(
        functools.partial(place_kernel, len(sources), pieces),
        out_shape=jax.ShapeDtypeStruct((sources[0].shape[0], columns), jnp.bfloat16),
        in_specs=[pl.BlockSpec(memory_space=pltpu.SMEM)]
        + [pl.BlockSpec(memory_space=pltpu.VMEM)] * len(sources)
        + [pl.BlockSpec(memory_space=pl.ANY)] * len(held),
        out_specs=pl.BlockSpec(memory_space=pl.ANY),
        scratch_shapes=[pltpu.SemaphoreType.DMA((len(sources) * len(pieces),))],
        input_output_aliases={1 + len(sources): 0} if held else {},
        compiler_params=pltpu.CompilerParams(vmem_limit_bytes=SMALL_VMEM),
        name=name,
    )(where, *sources, *held)


def per_device(
    tokens, inner_q, inner_k, inner_v, outer_q, outer_k, outer_v, moment_q, moment_k, value_momentum
):
    count = lax.axis_size("replica")
    n = lax.axis_size("fsdp")
    me = lax.axis_index("replica")
    row = lax.axis_index("fsdp")
    inners = (inner_q[0], inner_k[0], inner_v[0])
    outers = (outer_q, outer_k, outer_v)
    moments = (moment_q, moment_k, value_momentum)
    widths = [m.shape[1] for m in moments]
    rows = outer_q.shape[0]
    mine = tokens.shape[0]
    total_width = sum(widths)
    cut = total_width // 2
    streams = (cut, total_width - cut)
    LAG, LEAD = 0, 1

    where = me.astype(jnp.int32).reshape(1)
    block = jax.ShapeDtypeStruct((rows, total_width), jnp.float32)
    buffers = [pltpu.VMEM((rows, w), a.dtype) for a, w in zip((*inners, *outers), widths * 2)]

    def half(distance, name, where):
        kernel = functools.partial(half_kernel, distance)
        return columns_call(kernel, name, where, (*inners, *outers), [block] * 2, buffers)

    far_pack, near_pack = pack(where, inners, widths, (3, 1), "pack_inner")
    far_sibling = from_replica(far_pack, 1)
    near_sibling = from_replica(near_pack, 1)
    far_half, far_outer = half(2, "far_half", where)
    far = far_half + (far_outer - far_sibling.astype(jnp.float32))
    fars = [far[:, :cut].astype(jnp.bfloat16), far[:, cut:].astype(jnp.bfloat16)]
    remotes = [from_replica(f, 2) for f in fars]
    near_half, own_outer = half(0, "near_half", after(where, fars[LEAD]))

    tokens_1 = from_replica(tokens, 1)
    near_tokens = jnp.concatenate([tokens, tokens_1], axis=0)
    parts = (near_half, own_outer, near_sibling)
    fresh = [
        fresh_columns(*parts, after(remotes[LAG], near_tokens), moments, 0, count),
        fresh_columns(*parts, remotes[LEAD], moments, cut, count),
    ]
    tokens_2 = from_replica(after(tokens, remotes[LEAD]), 2)

    def whole_step(*others):
        remote = jnp.concatenate([after(remotes[0], *others), remotes[1]], axis=1)
        return own_step(*parts, remote, moments, count)

    up = [(ring_member(p, n), ring_member((p + 1) % n, n)) for p in range(n)]
    down = [(b, a) for a, b in up]
    last = n // 2

    def product(lhs, steps, first, block):
        lanes = lax.dynamic_slice_in_dim(lhs, source_of(row, steps, n) * rows + first, block.shape[0], 1)
        return jnp.dot(lanes, block, preferred_element_type=jnp.float32)

    near_outs, from_sibling = [None, None], [None, None]
    if n % 2 or not SHORTEST_RING <= n <= LONGEST_RING:
        gathered = [lax.all_gather(part, "fsdp", axis=0, tiled=True) for part in fresh]
        tokens_3 = from_replica(tokens_2, 1)
        far_tokens = jnp.concatenate([tokens_2, tokens_3], axis=0)
        delta, *new_moments = whole_step()
        delta_2 = from_replica(delta, 2)
        near_totals = [jnp.dot(near_tokens, g, preferred_element_type=jnp.float32) for g in gathered]
        far_totals = [jnp.dot(far_tokens, g, preferred_element_type=jnp.float32) for g in gathered]
    else:
        heads = [[part, part] for part in fresh]
        arrived = [[(0, 0, part)] for part in fresh]
        near_totals = [product(near_tokens, 0, 0, part) for part in fresh]
        far_totals = [None, None]

        def hop(stream, way, step, *others):
            heads[stream][way] = lax.ppermute(after(heads[stream][way], *others), "fsdp", (up, down)[way])
            arrived[stream].append((step if way == 0 else -step, 0, heads[stream][way]))

        def last_hop(stream, *others):
            for way, first, stop in ((0, 0, rows // 2), (1, rows // 2, rows)):
                part = after(heads[stream][way], *others)[first:stop]
                block = lax.ppermute(part, "fsdp", (up, down)[way])
                arrived[stream].append((last if way == 0 else -last, first, block))

        def add_near(stream, blocks):
            for block in blocks:
                near_totals[stream] += product(near_tokens, *block)

        def add_far(stream, blocks, *others):
            for steps, top, block in blocks:
                value = product(far_tokens, steps, top, after(block, *others) if others else block)
                far_totals[stream] = value if far_totals[stream] is None else far_totals[stream] + value

        def hold(stream, first, *others):
            arrived[stream][first:] = [(steps, top, after(b, *others)) for steps, top, b in arrived[stream][first:]]

        hop(LEAD, 0, 1)
        hop(LEAD, 1, 1)
        heads[LAG] = [after(block, *heads[LEAD]) for block in heads[LAG]]
        hop(LAG, 0, 1, near_totals[LAG])
        hop(LAG, 1, 1, near_totals[LAG])
        add_near(LEAD, arrived[LEAD][-2:])
        add_near(LAG, arrived[LAG][-2:])
        delta, *new_moments = whole_step(near_totals[LEAD])
        for step in range(2, last):
            for stream in (LEAD, LAG):
                hop(stream, 0, step, near_totals[stream])
                hop(stream, 1, step, near_totals[stream])
            if step < last - 1:
                add_near(LEAD, arrived[LEAD][-2:])
                add_near(LAG, arrived[LAG][-2:])
            if step == 2:
                tokens_2 = after(tokens_2, heads[LAG][0])
                tokens_3 = from_replica(tokens_2, 1)
                far_tokens = jnp.concatenate([tokens_2, tokens_3], axis=0)
                delta_2 = from_replica(after(delta, tokens_2), 2)
        add_near(LEAD, arrived[LEAD][-2:])
        last_hop(LEAD, near_totals[LEAD])
        add_far(LEAD, arrived[LEAD][:-2])
        hold(LAG, -2, far_totals[LEAD])
        add_near(LAG, arrived[LAG][-2:])
        hold(LEAD, -2, near_totals[LAG])
        add_near(LEAD, arrived[LEAD][-2:])
        add_far(LEAD, arrived[LEAD][-2:])
        near_outs[LEAD] = near_totals[LEAD].astype(jnp.bfloat16)
        from_sibling[LEAD] = from_replica(near_outs[LEAD][mine:], 1)
        last_hop(LAG, near_totals[LAG], from_sibling[LEAD])
        hold(LAG, -2, near_totals[LEAD], delta_2)
        add_far(LAG, arrived[LAG][:-2], from_sibling[LEAD], far_totals[LEAD])
        add_near(LAG, arrived[LAG][-2:])
        add_far(LAG, arrived[LAG][-2:], near_totals[LAG])

    held = [after(d, near_totals[LAG]) for d in (delta, delta_2)]
    pair = from_replica(jnp.concatenate(held, axis=1), 1)
    new_outers = subtract(where, outers, delta, delta_2, pair)

    base_k, base_v = count * widths[0], count * (widths[0] + widths[1])
    pieces = (
        ((0, widths[0], cut),),
        ((cut, widths[0], widths[0] - cut), (base_k, widths[1], widths[1]), (base_v, widths[2], widths[2])),
    )
    projected = None
    for stream, name in ((LEAD, "place_leading"), (LAG, "place_second")):
        if near_outs[stream] is None:
            near_outs[stream] = near_totals[stream].astype(jnp.bfloat16)
            from_sibling[stream] = from_replica(near_outs[stream][mine:], 1)
        far_out = far_totals[stream].astype(jnp.bfloat16)
        sources = [
            near_outs[stream][:mine],
            from_sibling[stream],
            from_replica(far_out[:mine], 2),
            from_replica(far_out[mine:], 3),
        ]
        if projected is not None:
            projected = after(projected, *new_outers)
        projected = place(where, sources, pieces[stream], count * total_width, projected, name)
    return projected, *new_outers, *new_moments


def solution(mesh):
    placed = (
        P(("replica", "fsdp"), None),
        P("replica", "fsdp", None),
        P("replica", "fsdp", None),
        P("replica", "fsdp", None),
        P("fsdp", None),
        P("fsdp", None),
        P("fsdp", None),
        P("fsdp", "replica"),
        P("fsdp", "replica"),
        P("fsdp", "replica"),
    )
    return jax.shard_map(
        per_device,
        mesh=mesh,
        in_specs=placed,
        out_specs=(
            P(("replica", "fsdp"), None),
            P("fsdp", None),
            P("fsdp", None),
            P("fsdp", None),
            P("fsdp", "replica"),
            P("fsdp", "replica"),
            P("fsdp", "replica"),
        ),
        check_vma=False,
    )
```

```python
import functools

import jax
import jax.numpy as jnp
from jax import lax
from jax.experimental import pallas as pl
from jax.experimental.pallas import tpu as pltpu
from jax.sharding import PartitionSpec as P

LEARN_RATE = 0.7
MOMENTUM_BETA = 0.9
SMALL_VMEM = 14 * 1024 * 1024
SHORTEST_RING = 8
LONGEST_RING = 16


def from_replica(x, distance):
    count = lax.axis_size("replica")
    return lax.ppermute(x, "replica", [(i, i ^ distance) for i in range(count)])


def ring_member(p, n):
    return 2 * p if p < n // 2 else 2 * (n - 1 - p) + 1


def source_of(row, steps, n):
    p = jnp.where(row % 2 == 0, row // 2, n - 1 - row // 2)
    p = (p - steps + n) % n
    return jnp.where(p < n // 2, 2 * p, 2 * (n - 1 - p) + 1)


def after(x, *others):
    return lax.optimization_barrier((x, *others))[0]


def fetch(sources, buffers, sems):
    copies = [pltpu.make_async_copy(a, b, sems.at[i]) for i, (a, b) in enumerate(zip(sources, buffers))]
    for copy in copies:
        copy.start()
    for copy in copies:
        copy.wait()


def columns_at(ref, block, width):
    return ref.at[:, pl.ds(pl.multiple_of(block * width, width), width)]


def in_hbm(arrays):
    return [pltpu.with_memory_space_constraint(a, pltpu.HBM) for a in arrays]


def spread(pieces, outs):
    edges = [0]
    for piece in pieces:
        edges.append(edges[-1] + piece.shape[1])
    left = 0
    for out in outs:
        right = left + out.shape[1]
        for piece, start in zip(pieces, edges):
            low, high = max(left, start), min(right, start + piece.shape[1])
            if low < high:
                out[:, low - left : high - left] = piece[:, low - start : high - start].astype(out.dtype)
        left = right


def columns_call(kernel, name, where, arrays, shapes, buffers):
    return pl.pallas_call(
        kernel,
        out_shape=shapes,
        in_specs=[pl.BlockSpec(memory_space=pltpu.SMEM)] + [pl.BlockSpec(memory_space=pl.ANY)] * len(arrays),
        out_specs=[pl.BlockSpec(memory_space=pltpu.VMEM)] * len(shapes),
        scratch_shapes=[*buffers, pltpu.SemaphoreType.DMA((len(arrays) * 2,))],
        compiler_params=pltpu.CompilerParams(vmem_limit_bytes=SMALL_VMEM),
        name=name,
    )(where, *in_hbm(arrays))


def pack_kernel(widths, distances, where, *refs):
    sources, outs, sems = refs[: len(widths)], refs[len(widths) : -1], refs[-1]
    views, targets = [], []
    for distance, out in zip(distances, outs):
        left = 0
        for source, width in zip(sources, widths):
            views.append(columns_at(source, lax.bitwise_xor(where[0], distance), width))
            targets.append(out.at[:, pl.ds(left, width)])
            left += width
    fetch(views, targets, sems)


def pack(where, arrays, widths, distances, name):
    shapes = [jax.ShapeDtypeStruct((arrays[0].shape[0], sum(widths)), arrays[0].dtype) for _ in distances]
    kernel = functools.partial(pack_kernel, widths, distances)
    return columns_call(kernel, name, where, arrays, shapes, [])


def half_kernel(distance, where, *refs):
    sources, outs, buffers, sems = refs[:6], refs[6:-7], refs[-7:-1], refs[-1]
    block = lax.bitwise_xor(where[0], distance)
    fetch([columns_at(r, block, b.shape[1]) for r, b in zip(sources, buffers)], buffers, sems)
    left = 0
    for inner, outer in zip(buffers[:3], buffers[3:]):
        columns = pl.ds(left, outer.shape[1])
        base = outer[...]
        outs[0][:, columns] = base - inner[...].astype(jnp.float32)
        outs[1][:, columns] = base
        left += outer.shape[1]


def own_kernel(count, half, outer, sibling, remote, moment_q, moment_k, moment_v, *outs):
    delta, new_moments = outs[0], outs[1:]
    left = 0
    for moment, new in zip((moment_q, moment_k, moment_v), new_moments):
        columns = pl.ds(left, moment.shape[1])
        own = half[:, columns] + (outer[:, columns] - sibling[:, columns].astype(jnp.float32))
        pseudo = (own + remote[:, columns].astype(jnp.float32)) / count
        new_moment = MOMENTUM_BETA * moment[...] + pseudo
        step = LEARN_RATE * (pseudo + MOMENTUM_BETA * new_moment)
        new[...] = new_moment
        delta[:, columns] = step.astype(jnp.bfloat16)
        left += moment.shape[1]


def own_step(half, outer, sibling, remote, moments, count):
    shapes = [jax.ShapeDtypeStruct(half.shape, jnp.bfloat16)]
    shapes += [jax.ShapeDtypeStruct(m.shape, jnp.float32) for m in moments]
    return pl.pallas_call(
        functools.partial(own_kernel, count),
        out_shape=shapes,
        in_specs=[pl.BlockSpec(memory_space=pltpu.VMEM)] * 7,
        out_specs=[pl.BlockSpec(memory_space=pltpu.VMEM)] * len(shapes),
        compiler_params=pltpu.CompilerParams(vmem_limit_bytes=SMALL_VMEM),
        name="own_step",
    )(half, outer, sibling, remote, *moments)


def fresh_kernel(count, first, half, outer, sibling, remote, moment_q, moment_k, moment_v, out):
    left, last = 0, first + out.shape[1]
    for moment in (moment_q, moment_k, moment_v):
        low, high = max(left, first), min(left + moment.shape[1], last)
        if low < high:
            columns = pl.ds(low, high - low)
            own = half[:, columns] + (outer[:, columns] - sibling[:, columns].astype(jnp.float32))
            pseudo = (own + remote[:, low - first : high - first].astype(jnp.float32)) / count
            new_moment = MOMENTUM_BETA * moment[:, low - left : high - left] + pseudo
            step = LEARN_RATE * (pseudo + MOMENTUM_BETA * new_moment)
            out[:, low - first : high - first] = (outer[:, columns] - step).astype(jnp.bfloat16)
        left += moment.shape[1]


def fresh_columns(half, outer, sibling, remote, moments, first, count):
    return pl.pallas_call(
        functools.partial(fresh_kernel, count, first),
        out_shape=jax.ShapeDtypeStruct(remote.shape, jnp.bfloat16),
        in_specs=[pl.BlockSpec(memory_space=pltpu.VMEM)] * 7,
        out_specs=pl.BlockSpec(memory_space=pltpu.VMEM),
        compiler_params=pltpu.CompilerParams(vmem_limit_bytes=SMALL_VMEM),
        name="fresh_columns",
    )(half, outer, sibling, remote, *moments)


def subtract_kernel(where, outer_q, outer_k, outer_v, own, remote, pair, *outs):
    outers = (outer_q, outer_k, outer_v)
    width = own.shape[1]
    deltas = (own, pair.at[:, pl.ds(0, width)], remote, pair.at[:, pl.ds(width, width)])
    for distance, delta in enumerate(deltas):
        block = lax.bitwise_xor(where[0], distance)
        start = 0
        for outer, out in zip(outers, outs):
            width = outer.shape[1] // len(deltas)
            columns = pl.ds(pl.multiple_of(block * width, width), width)
            out[:, columns] = outer[:, columns] - delta[:, start : start + width].astype(jnp.float32)
            start += width


def subtract(where, outers, own, remote, pair):
    return pl.pallas_call(
        subtract_kernel,
        out_shape=[jax.ShapeDtypeStruct(o.shape, o.dtype) for o in outers],
        in_specs=[pl.BlockSpec(memory_space=pltpu.SMEM)] + [pl.BlockSpec(memory_space=pltpu.VMEM)] * 6,
        out_specs=[pl.BlockSpec(memory_space=pltpu.VMEM)] * len(outers),
        compiler_params=pltpu.CompilerParams(vmem_limit_bytes=SMALL_VMEM),
        name="outer_minus_delta",
    )(where, *outers, own, remote, pair)


def place_kernel(count, pieces, where, *refs):
    sources, out, sems = refs[:count], refs[-2], refs[-1]
    copies = []
    for distance, source in enumerate(sources):
        block = lax.bitwise_xor(where[0], distance)
        left = 0
        for start, stride, width in pieces:
            at = pl.multiple_of(start + block * stride, 128)
            copies.append((source.at[:, pl.ds(left, width)], out.at[:, pl.ds(at, width)]))
            left += width
    fetch([a for a, _ in copies], [b for _, b in copies], sems)


def place(where, sources, pieces, columns, earlier, name):
    held = [] if earlier is None else [earlier]
    return pl.pallas_call(
        functools.partial(place_kernel, len(sources), pieces),
        out_shape=jax.ShapeDtypeStruct((sources[0].shape[0], columns), jnp.bfloat16),
        in_specs=[pl.BlockSpec(memory_space=pltpu.SMEM)]
        + [pl.BlockSpec(memory_space=pltpu.VMEM)] * len(sources)
        + [pl.BlockSpec(memory_space=pl.ANY)] * len(held),
        out_specs=pl.BlockSpec(memory_space=pl.ANY),
        scratch_shapes=[pltpu.SemaphoreType.DMA((len(sources) * len(pieces),))],
        input_output_aliases={1 + len(sources): 0} if held else {},
        compiler_params=pltpu.CompilerParams(vmem_limit_bytes=SMALL_VMEM),
        name=name,
    )(where, *sources, *held)


def per_device(
    tokens, inner_q, inner_k, inner_v, outer_q, outer_k, outer_v, moment_q, moment_k, value_momentum
):
    count = lax.axis_size("replica")
    n = lax.axis_size("fsdp")
    me = lax.axis_index("replica")
    row = lax.axis_index("fsdp")
    inners = (inner_q[0], inner_k[0], inner_v[0])
    outers = (outer_q, outer_k, outer_v)
    moments = (moment_q, moment_k, value_momentum)
    widths = [m.shape[1] for m in moments]
    rows = outer_q.shape[0]
    mine = tokens.shape[0]
    total_width = sum(widths)
    cut = total_width // 2
    streams = (cut, total_width - cut)
    LAG, LEAD = 0, 1

    where = me.astype(jnp.int32).reshape(1)
    block = jax.ShapeDtypeStruct((rows, total_width), jnp.float32)
    buffers = [pltpu.VMEM((rows, w), a.dtype) for a, w in zip((*inners, *outers), widths * 2)]

    def half(distance, name, where):
        kernel = functools.partial(half_kernel, distance)
        return columns_call(kernel, name, where, (*inners, *outers), [block] * 2, buffers)

    far_pack, near_pack = pack(where, inners, widths, (3, 1), "pack_inner")
    far_sibling = from_replica(far_pack, 1)
    near_sibling = from_replica(near_pack, 1)
    far_half, far_outer = half(2, "far_half", where)
    far = far_half + (far_outer - far_sibling.astype(jnp.float32))
    fars = [far[:, :cut].astype(jnp.bfloat16), far[:, cut:].astype(jnp.bfloat16)]
    remotes = [from_replica(f, 2) for f in fars]
    near_half, own_outer = half(0, "near_half", after(where, fars[LEAD]))

    tokens_1 = from_replica(tokens, 1)
    near_tokens = jnp.concatenate([tokens, tokens_1], axis=0)
    parts = (near_half, own_outer, near_sibling)
    fresh = [
        fresh_columns(*parts, after(remotes[LAG], near_tokens), moments, 0, count),
        fresh_columns(*parts, remotes[LEAD], moments, cut, count),
    ]
    tokens_2 = from_replica(after(tokens, remotes[LEAD]), 2)

    def whole_step(*others):
        remote = jnp.concatenate([after(remotes[0], *others), remotes[1]], axis=1)
        return own_step(*parts, remote, moments, count)

    up = [(ring_member(p, n), ring_member((p + 1) % n, n)) for p in range(n)]
    down = [(b, a) for a, b in up]
    last = n // 2

    def product(lhs, steps, first, block):
        lanes = lax.dynamic_slice_in_dim(lhs, source_of(row, steps, n) * rows + first, block.shape[0], 1)
        return jnp.dot(lanes, block, preferred_element_type=jnp.float32)

    near_outs, from_sibling = [None, None], [None, None]
    if n % 2 or not SHORTEST_RING <= n <= LONGEST_RING:
        gathered = [lax.all_gather(part, "fsdp", axis=0, tiled=True) for part in fresh]
        tokens_3 = from_replica(tokens_2, 1)
        far_tokens = jnp.concatenate([tokens_2, tokens_3], axis=0)
        delta, *new_moments = whole_step()
        delta_2 = from_replica(delta, 2)
        near_totals = [jnp.dot(near_tokens, g, preferred_element_type=jnp.float32) for g in gathered]
        far_totals = [jnp.dot(far_tokens, g, preferred_element_type=jnp.float32) for g in gathered]
    else:
        heads = [[part, part] for part in fresh]
        arrived = [[(0, 0, part)] for part in fresh]
        near_totals = [product(near_tokens, 0, 0, part) for part in fresh]
        far_totals = [None, None]

        def hop(stream, way, step, *others):
            heads[stream][way] = lax.ppermute(after(heads[stream][way], *others), "fsdp", (up, down)[way])
            arrived[stream].append((step if way == 0 else -step, 0, heads[stream][way]))

        def last_hop(stream, *others):
            for way, first, stop in ((0, 0, rows // 2), (1, rows // 2, rows)):
                part = after(heads[stream][way], *others)[first:stop]
                block = lax.ppermute(part, "fsdp", (up, down)[way])
                arrived[stream].append((last if way == 0 else -last, first, block))

        def add_near(stream, blocks):
            for block in blocks:
                near_totals[stream] += product(near_tokens, *block)

        def add_far(stream, blocks, *others):
            for steps, top, block in blocks:
                value = product(far_tokens, steps, top, after(block, *others) if others else block)
                far_totals[stream] = value if far_totals[stream] is None else far_totals[stream] + value

        def hold(stream, first, *others):
            arrived[stream][first:] = [(steps, top, after(b, *others)) for steps, top, b in arrived[stream][first:]]

        hop(LEAD, 0, 1)
        hop(LEAD, 1, 1)
        heads[LAG] = [after(block, *heads[LEAD]) for block in heads[LAG]]
        hop(LAG, 0, 1, near_totals[LAG])
        hop(LAG, 1, 1, near_totals[LAG])
        add_near(LEAD, arrived[LEAD][-2:])
        add_near(LAG, arrived[LAG][-2:])
        delta, *new_moments = whole_step(near_totals[LEAD])
        for step in range(2, last):
            for stream in (LEAD, LAG):
                hop(stream, 0, step, near_totals[stream])
                hop(stream, 1, step, near_totals[stream])
            if step < last - 1:
                add_near(LEAD, arrived[LEAD][-2:])
                add_near(LAG, arrived[LAG][-2:])
            if step == 2:
                tokens_2 = after(tokens_2, heads[LAG][0])
                tokens_3 = from_replica(tokens_2, 1)
                far_tokens = jnp.concatenate([tokens_2, tokens_3], axis=0)
                delta_2 = from_replica(after(delta, tokens_2), 2)
        add_near(LEAD, arrived[LEAD][-2:])
        last_hop(LEAD, near_totals[LEAD])
        add_far(LEAD, arrived[LEAD][:-2])
        hold(LAG, -2, far_totals[LEAD])
        add_near(LAG, arrived[LAG][-2:])
        hold(LEAD, -2, near_totals[LAG])
        add_near(LEAD, arrived[LEAD][-2:])
        add_far(LEAD, arrived[LEAD][-2:])
        near_outs[LEAD] = near_totals[LEAD].astype(jnp.bfloat16)
        from_sibling[LEAD] = from_replica(near_outs[LEAD][mine:], 1)
        last_hop(LAG, near_totals[LAG], from_sibling[LEAD])
        hold(LAG, -2, near_totals[LEAD], delta_2)
        add_far(LAG, arrived[LAG][:-2], from_sibling[LEAD], far_totals[LEAD])
        add_near(LAG, arrived[LAG][-2:])
        add_far(LAG, arrived[LAG][-2:], near_totals[LAG])

    held = [after(d, near_totals[LAG]) for d in (delta, delta_2)]
    pair = from_replica(jnp.concatenate(held, axis=1), 1)
    new_outers = subtract(where, outers, delta, delta_2, pair)

    base_k, base_v = count * widths[0], count * (widths[0] + widths[1])
    pieces = (
        ((0, widths[0], cut),),
        ((cut, widths[0], widths[0] - cut), (base_k, widths[1], widths[1]), (base_v, widths[2], widths[2])),
    )
    projected = None
    for stream, name in ((LEAD, "place_leading"), (LAG, "place_second")):
        if near_outs[stream] is None:
            near_outs[stream] = near_totals[stream].astype(jnp.bfloat16)
            from_sibling[stream] = from_replica(near_outs[stream][mine:], 1)
        far_out = far_totals[stream].astype(jnp.bfloat16)
        sources = [
            near_outs[stream][:mine],
            from_sibling[stream],
            from_replica(far_out[:mine], 2),
            from_replica(far_out[mine:], 3),
        ]
        if projected is not None:
            projected = after(projected, *new_outers)
        projected = place(where, sources, pieces[stream], count * total_width, projected, name)
    return projected, *new_outers, *new_moments


def solution(mesh):
    placed = (
        P(("replica", "fsdp"), None),
        P("replica", "fsdp", None),
        P("replica", "fsdp", None),
        P("replica", "fsdp", None),
        P("fsdp", None),
        P("fsdp", None),
        P("fsdp", None),
        P("fsdp", "replica"),
        P("fsdp", "replica"),
        P("fsdp", "replica"),
    )
    return jax.shard_map(
        per_device,
        mesh=mesh,
        in_specs=placed,
        out_specs=(
            P(("replica", "fsdp"), None),
            P("fsdp", None),
            P("fsdp", None),
            P("fsdp", None),
            P("fsdp", "replica"),
            P("fsdp", "replica"),
            P("fsdp", "replica"),
        ),
        check_vma=False,
    )
```
